32 devices in a mesh: groups: 2 (over y), tm: 16 (over z, x, core).
Axes of the slice: x: 2, y: 2, z: 4, core: 2. Of those that a mesh axis runs over, the one named last changes fastest.
Arguments:
- video: bfloat16 [32, 384, 1152], P(('groups', 'tm')), parts along dimension 0, may hold values from -6 to 6
- cam_len: int32 [32, 6], P(('groups', 'tm')), parts along dimension 0, may hold values from 16 to 64, as said below
- view_mask: int32 [6, 6], replicated, may hold values 0 or 1
- time_mask: int32 [8, 8], replicated, may hold values 0 or 1
- s_gain: float32 [1152], replicated, may hold values from 0.4 to 1.6
- t_gain: float32 [1152], replicated, may hold values from 0.4 to 1.6
- s_qkv: bfloat16 [1152, 1728], replicated, may hold values from -0.1875 to 0.1875
- s_out: bfloat16 [576, 1152], replicated, may hold values from -0.25 to 0.25
- t_qkv: bfloat16 [1152, 1728], replicated, may hold values from -0.1875 to 0.1875
- t_out: bfloat16 [576, 1152], replicated, may hold values from -0.25 to 0.25
- qk_gain: float32 [4, 72], replicated, as said below
Outputs:
- result: bfloat16 [32, 384, 1152], P(('groups', 'tm')), parts along dimension 0
The draws below stay inside these ranges and needn't reach their ends.
There are 2 independent parts, one for each index of `groups`. The reference program is written for one: setup_inputs(seed, part) draws one part's arguments, and reference() takes and returns one part's arrays. A program takes and returns all parts, laid end to end along the dimension named above; an argument that names none is the same for every part. Nothing has to cross between parts.
Inputs may be any that keep to these rules, and one draw needn't show every extreme that they name: `cam_len`: every frame has a camera with exactly 64 live tokens. `qk_gain`: positive gains.
All inputs are finite; a program needn't handle non-finite values.
Results may differ from the reference program's by a relative error of at most 0.02.
The reference program's roundings to bfloat16 on the way count: a program that leaves them out, or rounds other values in their place, can miss the bound.
Values may be sent and summed in bfloat16 or wider, within the bound.
A program may use at most 64 MiB of HBM per device.

```python
import jax
import jax.numpy as jnp
from jax import lax

C = 1152
HEADS = 8
HD = 72
CAMS = 6
TILE = 64
NBLK = 8
FRAMES = 16
N_TM = 16


def draw_cam_len(key, part):
    key = jax.random.fold_in(key, 11)
    first_key, second_key = jax.random.split(key)
    lengths = jax.random.randint(first_key, (FRAMES, CAMS), TILE // 4, TILE + 1)
    chosen = jax.random.randint(second_key, (FRAMES,), 0, CAMS)
    cameras = jnp.arange(CAMS, dtype=jnp.int32)
    return jnp.where(cameras[None, :] == chosen[:, None], TILE, lengths).astype(jnp.int32)


def draw_qk_gain(key, part):
    key = jax.random.fold_in(key, 23)
    gains = jax.random.uniform(key, (4, HD), jnp.float32, 0.7, 1.6)
    return gains


def plant(result, key, least, largest):
    spot = [jax.random.randint(jax.random.fold_in(key, axis), (), 0, length) for axis, length in enumerate(result.shape)]
    widest = result.shape.index(max(result.shape))
    next_to = spot[:widest] + [(spot[widest] + 1) % result.shape[widest]] + spot[widest + 1:]
    return result.at[tuple(spot)].set(least).at[tuple(next_to)].set(largest)


def shard_levels(key, extent, cuts, low, high):
    def one(dim, parts):
        heights = jax.random.uniform(jax.random.fold_in(jax.random.fold_in(key, 6), dim), (parts,), jnp.float32, low / len(cuts), high / len(cuts))
        return jnp.repeat(jnp.exp(heights), extent[dim] // parts).reshape((-1,) + (1,) * (len(extent) - dim - 1))

    factor_of = one(*cuts[0])
    for cut in cuts[1:]:
        factor_of = factor_of * one(*cut)
    return factor_of


def bell_draw(stream_key, dims, scale, bound, cuts=(), held_as=jnp.bfloat16):
    values = jax.random.normal(stream_key, dims, jnp.float32) * scale
    if len(cuts) > 0:
        values = shard_levels(stream_key, dims, cuts, -0.22, 0.18) * values
    return jnp.clip(values, min=-bound, max=bound).astype(held_as)


def setup_inputs(seed: int = 0, part: int = 0) -> dict:
    streams_of = jax.random.split(jax.random.key(seed), 12)
    part_splits = jax.random.split(jax.random.fold_in(streams_of[11], part), 12)
    return {
        "video": bell_draw(part_splits[0], (FRAMES, CAMS * TILE, C), 1.0, 6.0, ((0, 16),)),
        "cam_len": draw_cam_len(jax.random.fold_in(jax.random.fold_in(streams_of[11], part), 71), part),
        "view_mask": plant((jax.random.randint(streams_of[2], (CAMS, CAMS), 0, 2) < 1).astype(jnp.int32), jax.random.fold_in(streams_of[2], 1), 0, 1),
        "time_mask": plant((jax.random.randint(streams_of[3], (NBLK, NBLK), 0, 2) < 1).astype(jnp.int32), jax.random.fold_in(streams_of[3], 1), 0, 1),
        "s_gain": jnp.clip(1.0 + 0.12 * jax.random.normal(streams_of[4], (C,), jnp.float32), 0.4, 1.6),
        "t_gain": jnp.clip(1.0 + 0.12 * jax.random.normal(streams_of[5], (C,), jnp.float32), 0.4, 1.6),
        "s_qkv": bell_draw(streams_of[6], (C, 3 * HEADS * HD), C ** -0.5, 0.1875),
        "s_out": bell_draw(streams_of[7], (HEADS * HD, C), (HEADS * HD) ** -0.5, 0.25),
        "t_qkv": bell_draw(streams_of[8], (C, 3 * HEADS * HD), C ** -0.5, 0.1875),
        "t_out": bell_draw(streams_of[9], (HEADS * HD, C), (HEADS * HD) ** -0.5, 0.25),
        "qk_gain": draw_qk_gain(jax.random.fold_in(streams_of[11], 71), part),
    }


epsilon = 1e-06

def layer_norm(features, norm_gain):
    values_f = features.astype(jnp.float32)
    average = lax.optimization_barrier(jnp.mean(values_f, -1, keepdims=True))
    centred = values_f - average
    spread = lax.optimization_barrier(jnp.mean(centred * centred, -1, keepdims=True))
    return (centred * lax.rsqrt(spread + epsilon) * norm_gain).astype(jnp.bfloat16)

def qkv_heads(normed, matrix, qk_gains):
    leading = normed.shape[:-1]
    projected = jnp.dot(normed.reshape(-1, normed.shape[-1]), matrix, preferred_element_type=jnp.float32)
    projected = projected.reshape((-1, 3, HEADS, HD))
    queries = projected[:, 0]
    keys_part = projected[:, 1]
    values_part = projected[:, 2]
    queries = queries * lax.rsqrt(lax.optimization_barrier(jnp.mean(queries * queries, -1, keepdims=True)) + epsilon) * qk_gains[0]
    keys_part = keys_part * lax.rsqrt(lax.optimization_barrier(jnp.mean(keys_part * keys_part, -1, keepdims=True)) + epsilon) * qk_gains[1]
    packed = jnp.stack([queries, keys_part, values_part], 1).astype(jnp.bfloat16)
    return packed.reshape(leading + (3 * HEADS * HD,))

def softmax_rows(scores):
    highest = lax.optimization_barrier(jnp.max(scores, -1, keepdims=True))
    exponent = jnp.exp(scores - highest)
    return (exponent / lax.optimization_barrier(jnp.sum(exponent, -1, keepdims=True))).astype(jnp.bfloat16)

def spatial_frame(this_frame, lengths, view_mask, norm_gain, w_qkv, w_out, qk_gains):
    token_rows = this_frame.shape[0]
    tile_rows = token_rows // CAMS
    packed = qkv_heads(layer_norm(this_frame, norm_gain), w_qkv, qk_gains).reshape(token_rows, 3, HEADS, HD)
    ordinal = jnp.arange(token_rows, dtype=jnp.int32)
    camera = ordinal // tile_rows
    position = ordinal % tile_rows
    onehot = (camera[:, None] == jnp.arange(CAMS, dtype=jnp.int32)[None, :]).astype(jnp.float32)
    lengths_here = lax.optimization_barrier(jnp.sum(onehot * lengths.astype(jnp.float32)[None, :], 1))
    usable = position.astype(jnp.float32) < lengths_here
    linked = jnp.dot(jnp.dot(onehot, view_mask.astype(jnp.float32), precision=lax.Precision.HIGHEST), onehot.T, precision=lax.Precision.HIGHEST)
    allowed = ((linked > 0.5) | (camera[:, None] == camera[None, :])) & usable[None, :]
    scores = jnp.einsum('qhd,khd->hqk', packed[:, 0].astype(jnp.float32), packed[:, 1].astype(jnp.float32)) * HD ** (-0.5)
    scores = jnp.where(allowed[None], scores, -1e+30)
    weights = softmax_rows(scores)
    attended = jnp.einsum('hqk,khd->qhd', weights.astype(jnp.float32), packed[:, 2].astype(jnp.float32))
    attended = attended.astype(jnp.bfloat16).reshape(token_rows, HEADS * HD)
    projected = jnp.dot(attended, w_out, preferred_element_type=jnp.float32)
    return (this_frame.astype(jnp.float32) + projected).astype(jnp.bfloat16)

def frame_links(time_mask, frames):
    block_len = frames // NBLK
    expanded = jnp.repeat(jnp.repeat(time_mask, block_len, 0), block_len, 1) > 0
    ordinal = jnp.arange(frames, dtype=jnp.int32)
    earlier = ordinal[:, None] > ordinal[None, :]
    return expanded & earlier

def temporal_block(packed, usable, links):
    frames, item_count = (packed.shape[0], packed.shape[1])
    pieces = packed.reshape(frames, item_count, 3, HEADS, HD)
    scores = jnp.einsum('fmhd,gmhd->mhfg', pieces[:, :, 0].astype(jnp.float32), pieces[:, :, 1].astype(jnp.float32)) * HD ** (-0.5)
    ordinal = jnp.arange(frames, dtype=jnp.int32)
    diagonal = ordinal[:, None] == ordinal[None, :]
    allowed = diagonal[None] | links[None] & usable.T[:, None, :]
    scores = jnp.where(allowed[:, None], scores, -1e+30)
    weights = softmax_rows(scores)
    attended = jnp.einsum('mhfg,gmhd->fmhd', weights.astype(jnp.float32), pieces[:, :, 2].astype(jnp.float32))
    return attended.astype(jnp.bfloat16).reshape(frames, item_count, HEADS * HD)

def reference(video, cam_len, view_mask, time_mask, s_gain, t_gain, s_qkv, s_out, t_qkv, t_out, qk_gain):
    frames, token_rows, model_width = video.shape
    after_space = lax.map(lambda inputs_pair: spatial_frame(inputs_pair[0], inputs_pair[1], view_mask, s_gain, s_qkv, s_out, qk_gain[0:2]), (video, cam_len))
    tile_rows = token_rows // CAMS
    ordinal = jnp.arange(token_rows, dtype=jnp.int32)
    lengths_all = cam_len[:, ordinal // tile_rows]
    usable = (ordinal % tile_rows)[None, :] < lengths_all
    packed = qkv_heads(layer_norm(after_space, t_gain), t_qkv, qk_gain[2:4])
    per_peer = token_rows // N_TM
    blocks = token_rows // per_peer
    packed_blocks = packed.reshape(frames, blocks, per_peer, -1).transpose(1, 0, 2, 3)
    usable_blocks = usable.reshape(frames, blocks, per_peer).transpose(1, 0, 2)
    links = frame_links(time_mask, frames)
    attended = lax.map(lambda inputs_pair: temporal_block(inputs_pair[0], inputs_pair[1], links), (packed_blocks, usable_blocks))
    attended = attended.transpose(1, 0, 2, 3).reshape(frames * token_rows, HEADS * HD)
    projected = jnp.dot(attended, t_out, preferred_element_type=jnp.float32).astype(jnp.bfloat16)
    projected = projected.reshape(frames, token_rows, model_width)
    return (after_space.astype(jnp.float32) + projected.astype(jnp.float32)).astype(jnp.bfloat16)
```

```python
import functools

import jax
import jax.numpy as jnp
from jax import lax
from jax.experimental import pallas as pl
from jax.experimental.pallas import tpu as pltpu
from jax.sharding import PartitionSpec as P

HEADS = 8
HD = 72
CAMS = 6
NBLK = 8
UNIT = 16
ROWS = 128
LANES = 128
EPS = 1e-06
SCALE = HD ** (-0.5)
NEG = -1e30
F32, BF16, I32 = jnp.float32, jnp.bfloat16, jnp.int32


def normalize(values, gain):
    average = jnp.mean(values, -1, keepdims=True)
    centred = values - average
    spread = jnp.mean(centred * centred, -1, keepdims=True)
    return (centred * lax.rsqrt(spread + EPS) * gain).astype(BF16)


def split_sum(values, table):
    high = values.astype(BF16)
    low = (values - high.astype(F32)).astype(BF16)
    return jnp.dot(high, table, preferred_element_type=F32) + jnp.dot(
        low, table, preferred_element_type=F32
    )


def project(rows, weight, gain, sums, spreads, q_ref, k_ref, v_ref, at):
    width = HEADS * HD
    packed = jnp.dot(rows, weight[...], preferred_element_type=F32)
    qk = packed[:, : 2 * width]
    total = split_sum(qk * qk, sums[...])
    inverse = lax.rsqrt(total * (1.0 / HD) + EPS)
    high = inverse.astype(BF16).astype(F32)
    lane = lax.broadcasted_iota(I32, inverse.shape, 1)
    both = jnp.where(lane < 2 * HEADS, high, inverse - high).astype(BF16)
    spread = jnp.dot(both, spreads[...], preferred_element_type=F32)
    normed = (qk * spread * gain).astype(BF16)
    q_ref[at, :width] = normed[:, :width]
    k_ref[at, :width] = normed[:, width:]
    v_ref[at, :width] = packed[:, 2 * width :].astype(BF16)


def attend(q_ref, k_ref, v_ref, q_at, k_at, bias):
    tiles = [None] * (-(-HEADS * HD // LANES))
    for head in range(HEADS):
        first, last = head * HD // LANES, ((head + 1) * HD - 1) // LANES
        window = slice(first * LANES, (last + 1) * LANES)
        lane = lax.broadcasted_iota(I32, (1, (last + 1 - first) * LANES), 1) + first * LANES
        inside = (lane >= head * HD) & (lane < (head + 1) * HD)
        queries = q_ref[q_at, window] * jnp.where(inside, 1.0, 0.0).astype(BF16)
        scores = lax.dot_general(
            queries, k_ref[k_at, window], (((1,), (1,)), ((), ())), preferred_element_type=F32
        )
        scores = scores * SCALE + bias
        exponent = jnp.exp(scores - jnp.max(scores, -1, keepdims=True))
        weights = exponent * (1.0 / jnp.sum(exponent, -1, keepdims=True))
        part = jnp.dot(weights.astype(BF16), v_ref[k_at, window], preferred_element_type=F32)
        part = jnp.where(inside, part, 0.0)
        for tile in range(first, last + 1):
            piece = part[:, (tile - first) * LANES : (tile - first + 1) * LANES]
            tiles[tile] = piece if tiles[tile] is None else tiles[tile] + piece
    return jnp.concatenate(tiles, 1).astype(BF16)


def kernel(
    n,
    cam_len,
    view_mask,
    time_mask,
    video,
    cam_row,
    s_gain,
    t_gain,
    s_qk,
    t_qk,
    s_qkv_hbm,
    s_out_hbm,
    t_qkv_hbm,
    t_out_hbm,
    out,
    s_qkv,
    s_out,
    t_qkv,
    t_out,
    sums,
    spreads,
    sq,
    sk,
    sv,
    tq,
    tk,
    tv,
    after,
    sending,
    received,
    attended,
    returned,
    cams_all,
    links,
    weight_sem,
    cam_send,
    cam_recv,
    go_send,
    go_recv,
    back_send,
    back_recv,
):
    slots, model = after.shape
    width = HEADS * HD
    third = slots // (3 * UNIT)
    stride = (n // 2) // third
    me = lax.axis_index("tm")
    my_chip, my_core = me // 2, me % 2
    my_item = my_chip // stride
    working = (my_chip % stride) == 0
    my_units = jnp.where(working, 2 - my_core, 0)
    other = lax.rem(me + 1, n)

    loads = [
        pltpu.make_async_copy(src, dst, weight_sem.at[i])
        for i, (src, dst) in enumerate(
            ((s_qkv_hbm, s_qkv), (s_out_hbm, s_out), (t_qkv_hbm, t_qkv), (t_out_hbm, t_out))
        )
    ]
    for load in loads:
        load.start()

    barrier = pltpu.get_barrier_semaphore()

    def greet(step, carry):
        peer = lax.rem(me + step, n)
        pl.semaphore_signal(
            barrier, inc=1, device_id={"tm": peer}, device_id_type=pl.DeviceIdType.MESH
        )
        return carry

    lax.fori_loop(1, n, greet, 0)

    entry = lax.broadcasted_iota(I32, sums.shape, 0)
    head = lax.broadcasted_iota(I32, sums.shape, 1)
    head = jnp.where(head < 2 * HEADS, head, head - 2 * HEADS) * HD
    sums[...] = jnp.where((entry >= head) & (entry < head + HD), 1.0, 0.0).astype(BF16)
    entry = lax.broadcasted_iota(I32, spreads.shape, 1)
    head = lax.broadcasted_iota(I32, spreads.shape, 0)
    head = jnp.where(head < 2 * HEADS, head, head - 2 * HEADS) * HD
    spreads[...] = jnp.where((entry >= head) & (entry < head + HD), 1.0, 0.0).astype(BF16)
    for ref in (sq, sk, sv, tq, tk, tv):
        ref[:, width:] = jnp.zeros((ref.shape[0], ref.shape[1] - width), BF16)

    def to_normed(step, carry):
        at = pl.ds(pl.multiple_of(step * 64, 64), 64)
        sending[at, :] = normalize(video[0, at, :].astype(F32), s_gain[...])
        return carry

    lax.fori_loop(0, slots // 64, to_normed, 0)
    loads[0].wait()

    def to_heads(step, carry):
        at = pl.ds(pl.multiple_of(step * ROWS, ROWS), ROWS)
        project(sending[at, :], s_qkv, s_qk[...], sums, spreads, sq, sk, sv, at)
        return carry

    lax.fori_loop(0, slots // ROWS, to_heads, 0)

    pl.semaphore_wait(barrier, n - 1)

    def device_of(item, core):
        return item * (2 * stride) + core

    def cam_copy(item, core, frame):
        return pltpu.make_async_remote_copy(
            src_ref=cam_row,
            dst_ref=cams_all.at[frame],
            send_sem=cam_send.at[core, item],
            recv_sem=cam_recv.at[frame],
            device_id={"tm": device_of(item, core)},
            device_id_type=pl.DeviceIdType.MESH,
        )

    for core in range(2):

        def send_cams(item, carry):
            @pl.when(device_of(item, core) != me)
            def _():
                cam_copy(item, core, me).start()

            return carry

        lax.fori_loop(0, third, send_cams, 0)

    def go_copy(part, item, frame):
        core, slot = (1, 0) if part == 1 else (0, part // 2)
        at = pl.ds(pl.multiple_of((part * third + item) * UNIT, UNIT), UNIT)
        return pltpu.make_async_remote_copy(
            src_ref=sending.at[at],
            dst_ref=received.at[slot, pl.ds(pl.multiple_of(frame * UNIT, UNIT), UNIT)],
            send_sem=go_send.at[part, item],
            recv_sem=go_recv.at[slot, frame],
            device_id={"tm": device_of(item, core)},
            device_id_type=pl.DeviceIdType.MESH,
        )

    camera = lax.broadcasted_iota(I32, (1, slots), 1)
    tile = slots // CAMS
    length = jnp.zeros((1, slots), I32)
    for cam in range(CAMS):
        length = jnp.where(
            (camera >= cam * tile) & (camera < (cam + 1) * tile), cam_len[0, cam] + cam * tile, length
        )
    live = camera < length

    def camera_bias(query):
        seen = jnp.zeros((1, slots), I32)
        for cam in range(CAMS):
            mark = jnp.int32(1) if cam == query else view_mask[query, cam]
            seen = jnp.where((camera >= cam * tile) & (camera < (cam + 1) * tile), mark, seen)
        row = jnp.where((seen > 0) & live, 0.0, NEG)
        return jnp.broadcast_to(row, (tile, slots))

    loads[1].wait()
    per = ROWS // tile
    for part in range(3):
        at = pl.ds(part * ROWS, ROWS)
        bias = jnp.concatenate([camera_bias(part * per + i) for i in range(per)], 0)
        heads = attend(sq, sk, sv, at, slice(None), bias)[:, :width]
        mixed = jnp.dot(heads, s_out[...], preferred_element_type=F32)
        after_space = (video[0, at, :].astype(F32) + mixed).astype(BF16)
        after[at, :] = after_space
        sending[at, :] = normalize(after_space.astype(F32), t_gain[...])
        core, slot = (1, 0) if part == 1 else (0, part // 2)

        def send_part(step, carry):
            item = lax.rem(my_item + step, third)

            @pl.when(device_of(item, core) != me)
            def _():
                go_copy(part, item, me).start()

            return carry

        lax.fori_loop(0, third, send_part, 0)

        @pl.when(working & (my_core == core))
        def _():
            own = pl.ds(pl.multiple_of((part * third + my_item) * UNIT, UNIT), UNIT)
            received[slot, pl.ds(pl.multiple_of(me * UNIT, UNIT), UNIT), :] = sending[own, :]

    loads[2].wait()

    @pl.when(working)
    def _():
        cams_all[me] = cam_row[...]

        def cam_arrived(step, carry):
            cam_copy(0, 0, lax.rem(me + step, n)).wait_recv()
            return carry

        lax.fori_loop(1, n, cam_arrived, 0)

    span = n * UNIT
    block = span // NBLK

    def unit_of(slot):
        part = jnp.where(my_core == 1, 1, 2 * slot)
        return part * third + my_item

    def back_copy(slot, frame, unit):
        return pltpu.make_async_remote_copy(
            src_ref=attended.at[slot, pl.ds(pl.multiple_of(frame * UNIT, UNIT), UNIT)],
            dst_ref=returned.at[pl.ds(pl.multiple_of(unit * UNIT, UNIT), UNIT)],
            send_sem=back_send.at[slot, frame],
            recv_sem=back_recv.at[unit],
            device_id={"tm": frame},
            device_id_type=pl.DeviceIdType.MESH,
        )

    def work(slot, carry):
        unit = unit_of(slot)

        def arrived(step, inner):
            frame = lax.rem(me + step, n)
            pltpu.make_async_remote_copy(
                src_ref=sending.at[pl.ds(0, UNIT)],
                dst_ref=received.at[slot, pl.ds(pl.multiple_of(frame * UNIT, UNIT), UNIT)],
                send_sem=go_send.at[0, 0],
                recv_sem=go_recv.at[slot, frame],
                device_id={"tm": other},
                device_id_type=pl.DeviceIdType.MESH,
            ).wait_recv()
            return inner

        lax.fori_loop(1, n, arrived, 0)

        def heads_of(step, inner):
            at = pl.ds(pl.multiple_of(step * ROWS, ROWS), ROWS)
            project(received[slot, at, :], t_qkv, t_qk[...], sums, spreads, tq, tk, tv, at)
            return inner

        lax.fori_loop(0, span // ROWS, heads_of, 0)

        per_camera = tile // UNIT
        cam_lane = lax.broadcasted_iota(I32, (n, LANES), 1)
        cam_col = jnp.sum(
            jnp.where(cam_lane == unit // per_camera, cams_all[:, 0, :], 0), 1, keepdims=True
        )
        key = lax.broadcasted_iota(I32, (n, span), 1)
        begin = lax.broadcasted_iota(I32, (n, span), 0) * UNIT
        mine = (key >= begin) & (key < begin + UNIT)
        spot = key - begin + lax.rem(unit, per_camera) * UNIT
        usable = jnp.sum(jnp.where(mine & (spot < cam_col), 1.0, 0.0), 0, keepdims=True)
        column = lax.broadcasted_iota(I32, (1, span), 1)
        for query in range(NBLK):
            marks = jnp.zeros((1, span), I32)
            for other_block in range(NBLK):
                inside = (column >= other_block * block) & (column < (other_block + 1) * block)
                marks = jnp.where(inside, time_mask[query, other_block], marks)
            links[query : query + 1, :] = jnp.where(marks > 0, usable, 0.0)

        def mix(step, inner):
            at = pl.ds(pl.multiple_of(step * ROWS, ROWS), ROWS)
            row = lax.broadcasted_iota(I32, (ROWS, 1), 0) + step * ROWS
            mark = jnp.zeros((ROWS, span), F32)
            for query in range(NBLK):
                inside = (row >= query * block) & (row < (query + 1) * block)
                mark = jnp.where(inside, links[query : query + 1, :], mark)
            row_frame, column_frame = row // UNIT, column // UNIT
            same_slot = (row - row_frame * UNIT) == (column - column_frame * UNIT)
            earlier = (row_frame > column_frame) & (mark > 0.5)
            bias = jnp.where(same_slot & ((row_frame == column_frame) | earlier), 0.0, NEG)
            attended[slot, at, :] = attend(tq, tk, tv, at, slice(None), bias)[:, :width]
            return inner

        lax.fori_loop(0, span // ROWS, mix, 0)

        def send_back(step, inner):
            back_copy(slot, lax.rem(me + step, n), unit).start()
            return inner

        lax.fori_loop(1, n, send_back, 0)
        own = pl.ds(pl.multiple_of(me * UNIT, UNIT), UNIT)
        returned[pl.ds(pl.multiple_of(unit * UNIT, UNIT), UNIT), :] = attended[slot, own, :]
        return carry

    lax.fori_loop(0, my_units, work, 0)

    loads[3].wait()
    for part in range(3):
        core = 1 if part == 1 else 0

        def came_back(item, carry):
            @pl.when(device_of(item, core) != me)
            def _():
                unit = part * third + item
                pltpu.make_async_remote_copy(
                    src_ref=attended.at[0, pl.ds(0, UNIT)],
                    dst_ref=returned.at[pl.ds(pl.multiple_of(unit * UNIT, UNIT), UNIT)],
                    send_sem=back_send.at[0, 0],
                    recv_sem=back_recv.at[unit],
                    device_id={"tm": other},
                    device_id_type=pl.DeviceIdType.MESH,
                ).wait_recv()

            return carry

        lax.fori_loop(0, third, came_back, 0)
        at = pl.ds(part * ROWS, ROWS)
        mixed = jnp.dot(returned[at, :], t_out[...], preferred_element_type=F32).astype(BF16)
        out[0, at, :] = (after[at, :].astype(F32) + mixed.astype(F32)).astype(BF16)

    for core in range(2):

        def cams_sent(item, carry):
            @pl.when(device_of(item, core) != me)
            def _():
                cam_copy(item, core, me).wait_send()

            return carry

        lax.fori_loop(0, third, cams_sent, 0)
    for part in range(3):
        core = 1 if part == 1 else 0

        def part_sent(item, carry):
            @pl.when(device_of(item, core) != me)
            def _():
                go_copy(part, item, me).wait_send()

            return carry

        lax.fori_loop(0, third, part_sent, 0)

    def unit_sent(slot, carry):
        def frame_sent(step, inner):
            back_copy(slot, lax.rem(me + step, n), unit_of(slot)).wait_send()
            return inner

        return lax.fori_loop(1, n, frame_sent, carry)

    lax.fori_loop(0, my_units, unit_sent, 0)


def body(
    n, video, cam_len, view_mask, time_mask, s_gain, t_gain, s_qkv, s_out, t_qkv, t_out, qk_gain
):
    _, slots, model = video.shape
    width = HEADS * HD
    padded = -(-width // LANES) * LANES
    span = n * UNIT
    third = slots // (3 * UNIT)
    cam_row = jnp.broadcast_to(
        jnp.pad(cam_len, ((0, 0), (0, LANES - cam_len.shape[1]))), (8, LANES)
    )
    gains = jnp.broadcast_to(qk_gain[:, None, :], (4, HEADS, HD)).reshape(2, 1, 2 * width)
    smem = pl.BlockSpec(memory_space=pltpu.SMEM)
    vmem = pl.BlockSpec(memory_space=pltpu.VMEM)
    hbm = pl.BlockSpec(memory_space=pl.ANY)
    dma = pltpu.SemaphoreType.DMA
    return pl.pallas_call(
        functools.partial(kernel, n),
        out_shape=jax.ShapeDtypeStruct(video.shape, BF16),
        in_specs=[smem] * 3 + [vmem] * 6 + [hbm] * 4,
        out_specs=vmem,
        scratch_shapes=[
            pltpu.VMEM(s_qkv.shape, BF16),
            pltpu.VMEM(s_out.shape, BF16),
            pltpu.VMEM(t_qkv.shape, BF16),
            pltpu.VMEM(t_out.shape, BF16),
            pltpu.VMEM((2 * width, LANES), BF16),
            pltpu.VMEM((LANES, 2 * width), BF16),
            *[pltpu.VMEM((slots, padded), BF16)] * 3,
            *[pltpu.VMEM((span, padded), BF16)] * 3,
            pltpu.VMEM((slots, model), BF16),
            pltpu.VMEM((slots, model), BF16),
            pltpu.VMEM((2, span, model), BF16),
            pltpu.VMEM((2, span, width), BF16),
            pltpu.VMEM((slots, width), BF16),
            pltpu.VMEM((n, 8, LANES), I32),
            pltpu.VMEM((NBLK, span), F32),
            dma((4,)),
            dma((2, third)),
            dma((n,)),
            dma((3, third)),
            dma((2, n)),
            dma((2, n)),
            dma((3 * third,)),
        ],
        compiler_params=pltpu.CompilerParams(
            collective_id=0, has_side_effects=True, vmem_limit_bytes=58 * 1024 * 1024
        ),
        cost_estimate=pl.CostEstimate(
            flops=6_000_000_000, bytes_accessed=13_000_000, transcendentals=2_400_000
        ),
    )(
        cam_len,
        view_mask,
        time_mask,
        video,
        cam_row,
        s_gain[None],
        t_gain[None],
        gains[0],
        gains[1],
        s_qkv,
        s_out,
        t_qkv,
        t_out,
    )


def solution(mesh):
    placed = (P(("groups", "tm"), None, None), P(("groups", "tm"), None)) + (P(),) * 9
    return jax.shard_map(
        functools.partial(body, mesh.shape["tm"]),
        mesh=mesh,
        in_specs=placed,
        out_specs=P(("groups", "tm"), None, None),
        check_vma=False,
    )
```

```python
import functools

import jax
import jax.numpy as jnp
from jax import lax
from jax.experimental import pallas as pl
from jax.experimental.pallas import tpu as pltpu
from jax.sharding import PartitionSpec as P

HEADS = 8
HD = 72
CAMS = 6
NBLK = 8
UNIT = 16
ROWS = 128
LANES = 128
EPS = 1e-06
SCALE = HD ** (-0.5)
NEG = -1e30
F32, BF16, I32 = jnp.float32, jnp.bfloat16, jnp.int32


def normalize(values, gain):
    average = jnp.mean(values, -1, keepdims=True)
    centred = values - average
    spread = jnp.mean(centred * centred, -1, keepdims=True)
    return (centred * lax.rsqrt(spread + EPS) * gain).astype(BF16)


def split_sum(values, table):
    high = values.astype(BF16)
    low = (values - high.astype(F32)).astype(BF16)
    return jnp.dot(high, table, preferred_element_type=F32) + jnp.dot(
        low, table, preferred_element_type=F32
    )


def project(rows, weight, gain, sums, spreads, q_ref, k_ref, v_ref, at):
    width = HEADS * HD
    packed = lax.dot_general(
        rows, weight[...], (((1,), (1,)), ((), ())), preferred_element_type=F32
    )
    qk = packed[:, : 2 * width]
    total = split_sum(qk * qk, sums[...])
    inverse = lax.rsqrt(total * (1.0 / HD) + EPS)
    high = inverse.astype(BF16).astype(F32)
    lane = lax.broadcasted_iota(I32, inverse.shape, 1)
    both = jnp.where(lane < 2 * HEADS, high, inverse - high).astype(BF16)
    spread = jnp.dot(both, spreads[...], preferred_element_type=F32)
    normed = (qk * spread * gain).astype(BF16)
    q_ref[at, :width] = normed[:, :width]
    k_ref[at, :width] = normed[:, width:]
    v_ref[at, :width] = packed[:, 2 * width :].astype(BF16)


def attend(q_ref, k_ref, v_ref, q_at, k_at, bias):
    tiles = [None] * (-(-HEADS * HD // LANES))
    for head in range(HEADS):
        first, last = head * HD // LANES, ((head + 1) * HD - 1) // LANES
        window = slice(first * LANES, (last + 1) * LANES)
        lane = lax.broadcasted_iota(I32, (1, (last + 1 - first) * LANES), 1) + first * LANES
        inside = (lane >= head * HD) & (lane < (head + 1) * HD)
        queries = q_ref[q_at, window] * jnp.where(inside, 1.0, 0.0).astype(BF16)
        scores = lax.dot_general(
            queries, k_ref[k_at, window], (((1,), (1,)), ((), ())), preferred_element_type=F32
        )
        scores = scores * SCALE + bias
        exponent = jnp.exp(scores - jnp.max(scores, -1, keepdims=True))
        weights = exponent * (1.0 / jnp.sum(exponent, -1, keepdims=True))
        part = jnp.dot(weights.astype(BF16), v_ref[k_at, window], preferred_element_type=F32)
        part = jnp.where(inside, part, 0.0)
        for tile in range(first, last + 1):
            piece = part[:, (tile - first) * LANES : (tile - first + 1) * LANES]
            tiles[tile] = piece if tiles[tile] is None else tiles[tile] + piece
    return jnp.concatenate(tiles, 1).astype(BF16)


def kernel(
    n,
    cam_len,
    view_mask,
    time_mask,
    video,
    s_gain,
    t_gain,
    qk_gain,
    s_qkv_hbm,
    s_out_hbm,
    t_qkv_hbm,
    t_out_hbm,
    out,
    s_qkv,
    s_out,
    t_qkv,
    t_out,
    sums,
    spreads,
    sq,
    sk,
    sv,
    tq,
    tk,
    tv,
    after,
    sending,
    received,
    attended,
    returned,
    cam_row,
    cams_all,
    links,
    weight_sem,
    cam_send,
    cam_recv,
    go_send,
    go_recv,
    back_send,
    back_recv,
):
    slots, model = after.shape
    width = HEADS * HD
    third = slots // (3 * UNIT)
    stride = (n // 2) // third
    me = lax.axis_index("tm")
    my_chip, my_core = me // 2, me % 2
    my_item = my_chip // stride
    working = (my_chip % stride) == 0
    my_units = jnp.where(working, 2 - my_core, 0)
    other = lax.rem(me + 1, n)

    loads = [
        pltpu.make_async_copy(src, dst, weight_sem.at[i])
        for i, (src, dst) in enumerate(
            ((s_qkv_hbm, s_qkv), (s_out_hbm, s_out), (t_qkv_hbm, t_qkv), (t_out_hbm, t_out))
        )
    ]
    for load in loads:
        load.start()

    barrier = pltpu.get_barrier_semaphore()

    def greet(step, carry):
        peer = lax.rem(me + step, n)
        pl.semaphore_signal(
            barrier, inc=1, device_id={"tm": peer}, device_id_type=pl.DeviceIdType.MESH
        )
        return carry

    lax.fori_loop(1, n, greet, 0)

    entry = lax.broadcasted_iota(I32, sums.shape, 0)
    head = lax.broadcasted_iota(I32, sums.shape, 1)
    head = jnp.where(head < 2 * HEADS, head, head - 2 * HEADS) * HD
    sums[...] = jnp.where((entry >= head) & (entry < head + HD), 1.0, 0.0).astype(BF16)
    entry = lax.broadcasted_iota(I32, spreads.shape, 1)
    head = lax.broadcasted_iota(I32, spreads.shape, 0)
    head = jnp.where(head < 2 * HEADS, head, head - 2 * HEADS) * HD
    spreads[...] = jnp.where((entry >= head) & (entry < head + HD), 1.0, 0.0).astype(BF16)
    lane = lax.broadcasted_iota(I32, cam_row.shape, 1)
    lengths = jnp.zeros(cam_row.shape, I32)
    for cam in range(CAMS):
        lengths = jnp.where(lane == cam, cam_len[0, cam], lengths)
    cam_row[...] = lengths
    for ref in (sq, sk, sv, tq, tk, tv):
        ref[:, width:] = jnp.zeros((ref.shape[0], ref.shape[1] - width), BF16)

    def qk_row(first):
        pair = [qk_gain[first + i : first + i + 1, :] for i in range(2)]
        return jnp.concatenate([pair[0]] * HEADS + [pair[1]] * HEADS, 1)

    def to_normed(step, carry):
        at = pl.ds(pl.multiple_of(step * 64, 64), 64)
        sending[at, :] = normalize(video[0, at, :].astype(F32), s_gain[...][None, :])
        return carry

    lax.fori_loop(0, slots // 64, to_normed, 0)
    loads[0].wait()

    project(sending[...], s_qkv, qk_row(0), sums, spreads, sq, sk, sv, slice(None))

    pl.semaphore_wait(barrier, n - 1)

    def device_of(item, core):
        return item * (2 * stride) + core

    def cam_copy(item, core, frame):
        return pltpu.make_async_remote_copy(
            src_ref=cam_row,
            dst_ref=cams_all.at[frame],
            send_sem=cam_send.at[core, item],
            recv_sem=cam_recv.at[frame],
            device_id={"tm": device_of(item, core)},
            device_id_type=pl.DeviceIdType.MESH,
        )

    for core in range(2):

        def send_cams(item, carry):
            @pl.when(device_of(item, core) != me)
            def _():
                cam_copy(item, core, me).start()

            return carry

        lax.fori_loop(0, third, send_cams, 0)

    def go_copy(part, item, frame):
        core, slot = (1, 0) if part == 1 else (0, part // 2)
        at = pl.ds(pl.multiple_of((part * third + item) * UNIT, UNIT), UNIT)
        return pltpu.make_async_remote_copy(
            src_ref=sending.at[at],
            dst_ref=received.at[slot, pl.ds(pl.multiple_of(frame * UNIT, UNIT), UNIT)],
            send_sem=go_send.at[part, item],
            recv_sem=go_recv.at[slot, frame],
            device_id={"tm": device_of(item, core)},
            device_id_type=pl.DeviceIdType.MESH,
        )

    camera = lax.broadcasted_iota(I32, (1, slots), 1)
    tile = slots // CAMS
    length = jnp.zeros((1, slots), I32)
    for cam in range(CAMS):
        length = jnp.where(
            (camera >= cam * tile) & (camera < (cam + 1) * tile), cam_len[0, cam] + cam * tile, length
        )
    live = camera < length

    def camera_bias(query):
        seen = jnp.zeros((1, slots), I32)
        for cam in range(CAMS):
            mark = jnp.int32(1) if cam == query else view_mask[query, cam]
            seen = jnp.where((camera >= cam * tile) & (camera < (cam + 1) * tile), mark, seen)
        row = jnp.where((seen > 0) & live, 0.0, NEG)
        return jnp.broadcast_to(row, (tile, slots))

    loads[1].wait()
    per = ROWS // tile
    for part in range(3):
        at = pl.ds(part * ROWS, ROWS)
        bias = jnp.concatenate([camera_bias(part * per + i) for i in range(per)], 0)
        heads = attend(sq, sk, sv, at, slice(None), bias)[:, :width]
        mixed = jnp.dot(heads, s_out[...], preferred_element_type=F32)
        after_space = (video[0, at, :].astype(F32) + mixed).astype(BF16)
        after[at, :] = after_space
        sending[at, :] = normalize(after_space.astype(F32), t_gain[...][None, :])
        core, slot = (1, 0) if part == 1 else (0, part // 2)

        def send_part(step, carry):
            item = lax.rem(my_item + step, third)

            @pl.when(device_of(item, core) != me)
            def _():
                go_copy(part, item, me).start()

            return carry

        lax.fori_loop(0, third, send_part, 0)

        @pl.when(working & (my_core == core))
        def _():
            own = pl.ds(pl.multiple_of((part * third + my_item) * UNIT, UNIT), UNIT)
            received[slot, pl.ds(pl.multiple_of(me * UNIT, UNIT), UNIT), :] = sending[own, :]

    loads[2].wait()

    @pl.when(working)
    def _():
        cams_all[me] = cam_row[...]

        def cam_arrived(step, carry):
            cam_copy(0, 0, lax.rem(me + step, n)).wait_recv()
            return carry

        lax.fori_loop(1, n, cam_arrived, 0)

    span = n * UNIT
    block = span // NBLK

    def unit_of(slot):
        part = jnp.where(my_core == 1, 1, 2 * slot)
        return part * third + my_item

    def back_copy(slot, frame, unit):
        return pltpu.make_async_remote_copy(
            src_ref=attended.at[slot, pl.ds(pl.multiple_of(frame * UNIT, UNIT), UNIT)],
            dst_ref=returned.at[pl.ds(pl.multiple_of(unit * UNIT, UNIT), UNIT)],
            send_sem=back_send.at[slot, frame],
            recv_sem=back_recv.at[unit],
            device_id={"tm": frame},
            device_id_type=pl.DeviceIdType.MESH,
        )

    def work(slot, carry):
        unit = unit_of(slot)

        def arrived(step, inner):
            frame = lax.rem(me + step, n)
            pltpu.make_async_remote_copy(
                src_ref=sending.at[pl.ds(0, UNIT)],
                dst_ref=received.at[slot, pl.ds(pl.multiple_of(frame * UNIT, UNIT), UNIT)],
                send_sem=go_send.at[0, 0],
                recv_sem=go_recv.at[slot, frame],
                device_id={"tm": other},
                device_id_type=pl.DeviceIdType.MESH,
            ).wait_recv()
            return inner

        lax.fori_loop(1, n, arrived, 0)

        def heads_of(step, inner):
            at = pl.ds(pl.multiple_of(step * 2 * ROWS, ROWS), 2 * ROWS)
            project(received[slot, at, :], t_qkv, qk_row(2), sums, spreads, tq, tk, tv, at)
            return inner

        lax.fori_loop(0, span // (2 * ROWS), heads_of, 0)

        per_camera = tile // UNIT
        cam_lane = lax.broadcasted_iota(I32, (n, LANES), 1)
        cam_col = jnp.sum(
            jnp.where(cam_lane == unit // per_camera, cams_all[:, 0, :], 0), 1, keepdims=True
        )
        key = lax.broadcasted_iota(I32, (n, span), 1)
        begin = lax.broadcasted_iota(I32, (n, span), 0) * UNIT
        mine = (key >= begin) & (key < begin + UNIT)
        spot = key - begin + lax.rem(unit, per_camera) * UNIT
        usable = jnp.sum(jnp.where(mine & (spot < cam_col), 1.0, 0.0), 0, keepdims=True)
        column = lax.broadcasted_iota(I32, (1, span), 1)
        for query in range(NBLK):
            marks = jnp.zeros((1, span), I32)
            for other_block in range(NBLK):
                inside = (column >= other_block * block) & (column < (other_block + 1) * block)
                marks = jnp.where(inside, time_mask[query, other_block], marks)
            links[query : query + 1, :] = jnp.where(marks > 0, usable, 0.0)

        def mix(step, inner):
            at = pl.ds(pl.multiple_of(step * ROWS, ROWS), ROWS)
            row = lax.broadcasted_iota(I32, (ROWS, 1), 0) + step * ROWS
            mark = jnp.zeros((ROWS, span), F32)
            for query in range(NBLK):
                inside = (row >= query * block) & (row < (query + 1) * block)
                mark = jnp.where(inside, links[query : query + 1, :], mark)
            row_frame, column_frame = row // UNIT, column // UNIT
            same_slot = (row - row_frame * UNIT) == (column - column_frame * UNIT)
            earlier = (row_frame > column_frame) & (mark > 0.5)
            bias = jnp.where(same_slot & ((row_frame == column_frame) | earlier), 0.0, NEG)
            attended[slot, at, :] = attend(tq, tk, tv, at, slice(None), bias)[:, :width]
            return inner

        lax.fori_loop(0, span // ROWS, mix, 0)

        def send_back(step, inner):
            back_copy(slot, lax.rem(me + step, n), unit).start()
            return inner

        lax.fori_loop(1, n, send_back, 0)
        own = pl.ds(pl.multiple_of(me * UNIT, UNIT), UNIT)
        returned[pl.ds(pl.multiple_of(unit * UNIT, UNIT), UNIT), :] = attended[slot, own, :]
        return carry

    lax.fori_loop(0, my_units, work, 0)

    loads[3].wait()
    for part in range(3):
        core = 1 if part == 1 else 0

        def came_back(item, carry):
            @pl.when(device_of(item, core) != me)
            def _():
                unit = part * third + item
                pltpu.make_async_remote_copy(
                    src_ref=attended.at[0, pl.ds(0, UNIT)],
                    dst_ref=returned.at[pl.ds(pl.multiple_of(unit * UNIT, UNIT), UNIT)],
                    send_sem=back_send.at[0, 0],
                    recv_sem=back_recv.at[unit],
                    device_id={"tm": other},
                    device_id_type=pl.DeviceIdType.MESH,
                ).wait_recv()

            return carry

        lax.fori_loop(0, third, came_back, 0)
        at = pl.ds(part * ROWS, ROWS)
        mixed = jnp.dot(returned[at, :], t_out[...], preferred_element_type=F32).astype(BF16)
        out[0, at, :] = (after[at, :].astype(F32) + mixed.astype(F32)).astype(BF16)

    for core in range(2):

        def cams_sent(item, carry):
            @pl.when(device_of(item, core) != me)
            def _():
                cam_copy(item, core, me).wait_send()

            return carry

        lax.fori_loop(0, third, cams_sent, 0)
    for part in range(3):
        core = 1 if part == 1 else 0

        def part_sent(item, carry):
            @pl.when(device_of(item, core) != me)
            def _():
                go_copy(part, item, me).wait_send()

            return carry

        lax.fori_loop(0, third, part_sent, 0)

    def unit_sent(slot, carry):
        def frame_sent(step, inner):
            back_copy(slot, lax.rem(me + step, n), unit_of(slot)).wait_send()
            return inner

        return lax.fori_loop(1, n, frame_sent, carry)

    lax.fori_loop(0, my_units, unit_sent, 0)


def body(
    n, video, cam_len, view_mask, time_mask, s_gain, t_gain, s_qkv, s_out, t_qkv, t_out, qk_gain
):
    _, slots, model = video.shape
    width = HEADS * HD
    padded = -(-width // LANES) * LANES
    span = n * UNIT
    third = slots // (3 * UNIT)
    smem = pl.BlockSpec(memory_space=pltpu.SMEM)
    vmem = pl.BlockSpec(memory_space=pltpu.VMEM)
    hbm = pl.BlockSpec(memory_space=pl.ANY)
    dma = pltpu.SemaphoreType.DMA
    return pl.pallas_call(
        functools.partial(kernel, n),
        out_shape=jax.ShapeDtypeStruct(video.shape, BF16),
        in_specs=[smem] * 3 + [vmem] * 4 + [hbm] * 4,
        out_specs=vmem,
        scratch_shapes=[
            pltpu.VMEM(s_qkv.shape[::-1], BF16),
            pltpu.VMEM(s_out.shape, BF16),
            pltpu.VMEM(t_qkv.shape[::-1], BF16),
            pltpu.VMEM(t_out.shape, BF16),
            pltpu.VMEM((2 * width, LANES), BF16),
            pltpu.VMEM((LANES, 2 * width), BF16),
            *[pltpu.VMEM((slots, padded), BF16)] * 3,
            *[pltpu.VMEM((span, padded), BF16)] * 3,
            pltpu.VMEM((slots, model), BF16),
            pltpu.VMEM((slots, model), BF16),
            pltpu.VMEM((2, span, model), BF16),
            pltpu.VMEM((2, span, width), BF16),
            pltpu.VMEM((slots, width), BF16),
            pltpu.VMEM((8, LANES), I32),
            pltpu.VMEM((n, 8, LANES), I32),
            pltpu.VMEM((NBLK, span), F32),
            dma((4,)),
            dma((2, third)),
            dma((n,)),
            dma((3, third)),
            dma((2, n)),
            dma((2, n)),
            dma((3 * third,)),
        ],
        compiler_params=pltpu.CompilerParams(
            collective_id=0, has_side_effects=True, vmem_limit_bytes=58 * 1024 * 1024
        ),
        cost_estimate=pl.CostEstimate(
            flops=6_000_000_000, bytes_accessed=13_000_000, transcendentals=2_400_000
        ),
    )(
        cam_len,
        view_mask,
        time_mask,
        video,
        s_gain,
        t_gain,
        qk_gain,
        s_qkv.T,
        s_out,
        t_qkv.T,
        t_out,
    )


def solution(mesh):
    placed = (P(("groups", "tm"), None, None), P(("groups", "tm"), None)) + (P(),) * 9
    return jax.shard_map(
        functools.partial(body, mesh.shape["tm"]),
        mesh=mesh,
        in_specs=placed,
        out_specs=P(("groups", "tm"), None, None),
        check_vma=False,
    )
```

```python
import functools

import jax
import jax.numpy as jnp
from jax import lax
from jax.experimental import pallas as pl
from jax.experimental.pallas import tpu as pltpu
from jax.sharding import PartitionSpec as P

HEADS = 8
HD = 72
CAMS = 6
NBLK = 8
UNIT = 16
ROWS = 128
LANES = 128
EPS = 1e-06
SCALE = HD ** (-0.5)
NEG = -1e30
F32, BF16, I32 = jnp.float32, jnp.bfloat16, jnp.int32


def normalize(values, gain):
    average = jnp.mean(values, -1, keepdims=True)
    centred = values - average
    spread = jnp.mean(centred * centred, -1, keepdims=True)
    return (centred * lax.rsqrt(spread + EPS) * gain).astype(BF16)


def split_sum(values, table):
    high = values.astype(BF16)
    low = (values - high.astype(F32)).astype(BF16)
    return jnp.dot(high, table, preferred_element_type=F32) + jnp.dot(
        low, table, preferred_element_type=F32
    )


def project(rows, weight, gain, sums, spreads, q_ref, k_ref, v_ref, at):
    width = HEADS * HD
    packed = lax.dot_general(
        rows, weight[...], (((1,), (1,)), ((), ())), preferred_element_type=F32
    )
    qk = packed[:, : 2 * width]
    total = split_sum(qk * qk, sums[...])
    inverse = lax.rsqrt(total * (1.0 / HD) + EPS)
    high = inverse.astype(BF16).astype(F32)
    lane = lax.broadcasted_iota(I32, inverse.shape, 1)
    both = jnp.where(lane < 2 * HEADS, high, inverse - high).astype(BF16)
    spread = jnp.dot(both, spreads[...], preferred_element_type=F32)
    normed = (qk * spread * gain).astype(BF16)
    q_ref[at, :width] = normed[:, :width]
    k_ref[at, :width] = normed[:, width:]
    v_ref[at, :width] = packed[:, 2 * width :].astype(BF16)


def attend(q_ref, k_ref, v_ref, q_at, k_at, bias):
    tiles = [None] * (-(-HEADS * HD // LANES))
    group = HEADS if bias.shape[1] <= 512 else 2
    for begin in range(0, HEADS, group):
        views = []
        for head in range(begin, begin + group):
            first, last = head * HD // LANES, ((head + 1) * HD - 1) // LANES
            lane = lax.broadcasted_iota(I32, (1, (last + 1 - first) * LANES), 1) + first * LANES
            inside = (lane >= head * HD) & (lane < (head + 1) * HD)
            views.append((first, last, slice(first * LANES, (last + 1) * LANES), inside))
        scores = []
        for _, _, window, inside in views:
            queries = q_ref[q_at, window] * jnp.where(inside, 1.0, 0.0).astype(BF16)
            scores.append(
                lax.dot_general(
                    queries,
                    k_ref[k_at, window],
                    (((1,), (1,)), ((), ())),
                    preferred_element_type=F32,
                )
            )
        weights = []
        for score in scores:
            score = score * SCALE + bias
            exponent = jnp.exp(score - jnp.max(score, -1, keepdims=True))
            weights.append(
                (exponent * (1.0 / jnp.sum(exponent, -1, keepdims=True))).astype(BF16)
            )
        for weight, (first, last, window, inside) in zip(weights, views):
            part = jnp.dot(weight, v_ref[k_at, window], preferred_element_type=F32)
            part = jnp.where(inside, part, 0.0)
            for tile in range(first, last + 1):
                piece = part[:, (tile - first) * LANES : (tile - first + 1) * LANES]
                tiles[tile] = piece if tiles[tile] is None else tiles[tile] + piece
    return jnp.concatenate(tiles, 1).astype(BF16)


def kernel(
    n,
    cam_len,
    view_mask,
    time_mask,
    video,
    s_gain,
    t_gain,
    qk_gain,
    s_qkv_hbm,
    s_out_hbm,
    t_qkv_hbm,
    t_out_hbm,
    out,
    s_qkv,
    s_out,
    t_qkv,
    t_out,
    sums,
    spreads,
    sq,
    sk,
    sv,
    tq,
    tk,
    tv,
    after,
    sending,
    received,
    attended,
    returned,
    cam_row,
    cams_all,
    links,
    weight_sem,
    cam_send,
    cam_recv,
    go_send,
    go_recv,
    back_send,
    back_recv,
):
    slots, model = after.shape
    width = HEADS * HD
    third = slots // (3 * UNIT)
    stride = (n // 2) // third
    me = lax.axis_index("tm")
    my_chip, my_core = me // 2, me % 2
    my_item = my_chip // stride
    working = (my_chip % stride) == 0
    my_units = jnp.where(working, 2 - my_core, 0)
    other = lax.rem(me + 1, n)

    loads = [
        pltpu.make_async_copy(src, dst, weight_sem.at[i])
        for i, (src, dst) in enumerate(
            ((s_qkv_hbm, s_qkv), (s_out_hbm, s_out), (t_qkv_hbm, t_qkv), (t_out_hbm, t_out))
        )
    ]
    loads[0].start()

    barrier = pltpu.get_barrier_semaphore()

    def greet(step, carry):
        peer = lax.rem(me + step, n)
        pl.semaphore_signal(
            barrier, inc=1, device_id={"tm": peer}, device_id_type=pl.DeviceIdType.MESH
        )
        return carry

    lax.fori_loop(1, n, greet, 0)

    entry = lax.broadcasted_iota(I32, sums.shape, 0)
    head = lax.broadcasted_iota(I32, sums.shape, 1)
    head = jnp.where(head < 2 * HEADS, head, head - 2 * HEADS) * HD
    sums[...] = jnp.where((entry >= head) & (entry < head + HD), 1.0, 0.0).astype(BF16)
    entry = lax.broadcasted_iota(I32, spreads.shape, 1)
    head = lax.broadcasted_iota(I32, spreads.shape, 0)
    head = jnp.where(head < 2 * HEADS, head, head - 2 * HEADS) * HD
    spreads[...] = jnp.where((entry >= head) & (entry < head + HD), 1.0, 0.0).astype(BF16)
    lane = lax.broadcasted_iota(I32, cam_row.shape, 1)
    lengths = jnp.zeros(cam_row.shape, I32)
    for cam in range(CAMS):
        lengths = jnp.where(lane == cam, cam_len[0, cam], lengths)
    cam_row[...] = lengths
    for ref in (sq, sk, sv, tq, tk, tv):
        ref[:, width:] = jnp.zeros((ref.shape[0], ref.shape[1] - width), BF16)

    def qk_row(first):
        pair = [qk_gain[first + i : first + i + 1, :] for i in range(2)]
        return jnp.concatenate([pair[0]] * HEADS + [pair[1]] * HEADS, 1)

    def to_normed(step, carry):
        at = pl.ds(pl.multiple_of(step * 64, 64), 64)
        sending[at, :] = normalize(video[0, at, :].astype(F32), s_gain[...][None, :])
        return carry

    lax.fori_loop(0, slots // 64, to_normed, 0)
    loads[0].wait()
    for load in loads[1:]:
        load.start()

    project(sending[...], s_qkv, qk_row(0), sums, spreads, sq, sk, sv, slice(None))

    pl.semaphore_wait(barrier, n - 1)

    def device_of(item, core):
        return item * (2 * stride) + core

    def cam_copy(item, core, frame):
        return pltpu.make_async_remote_copy(
            src_ref=cam_row,
            dst_ref=cams_all.at[frame],
            send_sem=cam_send.at[core, item],
            recv_sem=cam_recv.at[frame],
            device_id={"tm": device_of(item, core)},
            device_id_type=pl.DeviceIdType.MESH,
        )

    for core in range(2):

        def send_cams(item, carry):
            @pl.when(device_of(item, core) != me)
            def _():
                cam_copy(item, core, me).start()

            return carry

        lax.fori_loop(0, third, send_cams, 0)

    def go_copy(part, item, frame):
        core, slot = (1, 0) if part == 1 else (0, part // 2)
        at = pl.ds(pl.multiple_of((part * third + item) * UNIT, UNIT), UNIT)
        return pltpu.make_async_remote_copy(
            src_ref=sending.at[at],
            dst_ref=received.at[slot, pl.ds(pl.multiple_of(frame * UNIT, UNIT), UNIT)],
            send_sem=go_send.at[part, item],
            recv_sem=go_recv.at[slot, frame],
            device_id={"tm": device_of(item, core)},
            device_id_type=pl.DeviceIdType.MESH,
        )

    camera = lax.broadcasted_iota(I32, (1, slots), 1)
    tile = slots // CAMS
    length = jnp.zeros((1, slots), I32)
    for cam in range(CAMS):
        length = jnp.where(
            (camera >= cam * tile) & (camera < (cam + 1) * tile), cam_len[0, cam] + cam * tile, length
        )
    live = camera < length

    def camera_bias(query):
        seen = jnp.zeros((1, slots), I32)
        for cam in range(CAMS):
            mark = jnp.int32(1) if cam == query else view_mask[query, cam]
            seen = jnp.where((camera >= cam * tile) & (camera < (cam + 1) * tile), mark, seen)
        row = jnp.where((seen > 0) & live, 0.0, NEG)
        return jnp.broadcast_to(row, (tile, slots))

    loads[1].wait()
    per = ROWS // tile
    for part in range(3):
        at = pl.ds(part * ROWS, ROWS)
        bias = jnp.concatenate([camera_bias(part * per + i) for i in range(per)], 0)
        heads = attend(sq, sk, sv, at, slice(None), bias)[:, :width]
        mixed = jnp.dot(heads, s_out[...], preferred_element_type=F32)
        after_space = (video[0, at, :].astype(F32) + mixed).astype(BF16)
        after[at, :] = after_space
        sending[at, :] = normalize(after_space.astype(F32), t_gain[...][None, :])
        core, slot = (1, 0) if part == 1 else (0, part // 2)

        def send_part(step, carry):
            near = third // 2
            half = my_item // near
            half = jnp.where(step < near, 1 - half, half)
            item = half * near + lax.rem(my_item + step, near)

            @pl.when(device_of(item, core) != me)
            def _():
                go_copy(part, item, me).start()

            return carry

        lax.fori_loop(0, third, send_part, 0)

        @pl.when(working & (my_core == core))
        def _():
            own = pl.ds(pl.multiple_of((part * third + my_item) * UNIT, UNIT), UNIT)
            received[slot, pl.ds(pl.multiple_of(me * UNIT, UNIT), UNIT), :] = sending[own, :]

    loads[2].wait()

    @pl.when(working)
    def _():
        cams_all[me] = cam_row[...]

        def cam_arrived(step, carry):
            cam_copy(0, 0, lax.rem(me + step, n)).wait_recv()
            return carry

        lax.fori_loop(1, n, cam_arrived, 0)

    span = n * UNIT
    block = span // NBLK

    def unit_of(slot):
        part = jnp.where(my_core == 1, 1, 2 * slot)
        return part * third + my_item

    def back_copy(slot, frame, unit):
        return pltpu.make_async_remote_copy(
            src_ref=attended.at[slot, pl.ds(pl.multiple_of(frame * UNIT, UNIT), UNIT)],
            dst_ref=returned.at[pl.ds(pl.multiple_of(unit * UNIT, UNIT), UNIT)],
            send_sem=back_send.at[slot, frame],
            recv_sem=back_recv.at[unit],
            device_id={"tm": frame},
            device_id_type=pl.DeviceIdType.MESH,
        )

    def work(slot, carry):
        unit = unit_of(slot)

        def arrived(step, inner):
            frame = lax.rem(me + step, n)
            pltpu.make_async_remote_copy(
                src_ref=sending.at[pl.ds(0, UNIT)],
                dst_ref=received.at[slot, pl.ds(pl.multiple_of(frame * UNIT, UNIT), UNIT)],
                send_sem=go_send.at[0, 0],
                recv_sem=go_recv.at[slot, frame],
                device_id={"tm": other},
                device_id_type=pl.DeviceIdType.MESH,
            ).wait_recv()
            return inner

        lax.fori_loop(1, n, arrived, 0)

        def heads_of(step, inner):
            at = pl.ds(pl.multiple_of(step * 2 * ROWS, ROWS), 2 * ROWS)
            project(received[slot, at, :], t_qkv, qk_row(2), sums, spreads, tq, tk, tv, at)
            return inner

        lax.fori_loop(0, span // (2 * ROWS), heads_of, 0)

        per_camera = tile // UNIT
        cam_lane = lax.broadcasted_iota(I32, (n, LANES), 1)
        cam_col = jnp.sum(
            jnp.where(cam_lane == unit // per_camera, cams_all[:, 0, :], 0), 1, keepdims=True
        )
        key = lax.broadcasted_iota(I32, (n, span), 1)
        begin = lax.broadcasted_iota(I32, (n, span), 0) * UNIT
        mine = (key >= begin) & (key < begin + UNIT)
        spot = key - begin + lax.rem(unit, per_camera) * UNIT
        usable = jnp.sum(jnp.where(mine & (spot < cam_col), 1.0, 0.0), 0, keepdims=True)
        column = lax.broadcasted_iota(I32, (1, span), 1)
        for query in range(NBLK):
            marks = jnp.zeros((1, span), I32)
            for other_block in range(NBLK):
                inside = (column >= other_block * block) & (column < (other_block + 1) * block)
                marks = jnp.where(inside, time_mask[query, other_block], marks)
            links[query : query + 1, :] = jnp.where(marks > 0, usable, 0.0)

        pieces = span // ROWS
        far = jnp.where(me < n // 2, pieces // 2, 0)

        def mix(step, inner):
            piece = lax.rem(step + far, pieces)
            at = pl.ds(pl.multiple_of(piece * ROWS, ROWS), ROWS)
            row = lax.broadcasted_iota(I32, (ROWS, 1), 0) + piece * ROWS
            mark = jnp.zeros((ROWS, span), F32)
            for query in range(NBLK):
                inside = (row >= query * block) & (row < (query + 1) * block)
                mark = jnp.where(inside, links[query : query + 1, :], mark)
            row_frame, column_frame = row // UNIT, column // UNIT
            same_slot = (row - row_frame * UNIT) == (column - column_frame * UNIT)
            earlier = (row_frame > column_frame) & (mark > 0.5)
            bias = jnp.where(same_slot & ((row_frame == column_frame) | earlier), 0.0, NEG)
            attended[slot, at, :] = attend(tq, tk, tv, at, slice(None), bias)[:, :width]
            frames = ROWS // UNIT

            def send_back(turn, deeper):
                frame = piece * frames + lax.rem(me + turn, frames)

                @pl.when(frame != me)
                def _():
                    back_copy(slot, frame, unit).start()

                return deeper

            return lax.fori_loop(0, frames, send_back, inner)

        lax.fori_loop(0, pieces, mix, 0)
        own = pl.ds(pl.multiple_of(me * UNIT, UNIT), UNIT)
        returned[pl.ds(pl.multiple_of(unit * UNIT, UNIT), UNIT), :] = attended[slot, own, :]
        return carry

    lax.fori_loop(0, my_units, work, 0)

    loads[3].wait()
    for part in range(3):
        core = 1 if part == 1 else 0

        def came_back(item, carry):
            @pl.when(device_of(item, core) != me)
            def _():
                unit = part * third + item
                pltpu.make_async_remote_copy(
                    src_ref=attended.at[0, pl.ds(0, UNIT)],
                    dst_ref=returned.at[pl.ds(pl.multiple_of(unit * UNIT, UNIT), UNIT)],
                    send_sem=back_send.at[0, 0],
                    recv_sem=back_recv.at[unit],
                    device_id={"tm": other},
                    device_id_type=pl.DeviceIdType.MESH,
                ).wait_recv()

            return carry

        lax.fori_loop(0, third, came_back, 0)
        at = pl.ds(part * ROWS, ROWS)
        mixed = jnp.dot(returned[at, :], t_out[...], preferred_element_type=F32).astype(BF16)
        out[0, at, :] = (after[at, :].astype(F32) + mixed.astype(F32)).astype(BF16)

    for core in range(2):

        def cams_sent(item, carry):
            @pl.when(device_of(item, core) != me)
            def _():
                cam_copy(item, core, me).wait_send()

            return carry

        lax.fori_loop(0, third, cams_sent, 0)
    for part in range(3):
        core = 1 if part == 1 else 0

        def part_sent(item, carry):
            @pl.when(device_of(item, core) != me)
            def _():
                go_copy(part, item, me).wait_send()

            return carry

        lax.fori_loop(0, third, part_sent, 0)

    def unit_sent(slot, carry):
        def frame_sent(step, inner):
            back_copy(slot, lax.rem(me + step, n), unit_of(slot)).wait_send()
            return inner

        return lax.fori_loop(1, n, frame_sent, carry)

    lax.fori_loop(0, my_units, unit_sent, 0)


def body(
    n, video, cam_len, view_mask, time_mask, s_gain, t_gain, s_qkv, s_out, t_qkv, t_out, qk_gain
):
    _, slots, model = video.shape
    width = HEADS * HD
    padded = -(-width // LANES) * LANES
    span = n * UNIT
    third = slots // (3 * UNIT)
    smem = pl.BlockSpec(memory_space=pltpu.SMEM)
    vmem = pl.BlockSpec(memory_space=pltpu.VMEM)
    hbm = pl.BlockSpec(memory_space=pl.ANY)
    dma = pltpu.SemaphoreType.DMA
    return pl.pallas_call(
        functools.partial(kernel, n),
        out_shape=jax.ShapeDtypeStruct(video.shape, BF16),
        in_specs=[smem] * 3 + [vmem] * 4 + [hbm] * 4,
        out_specs=vmem,
        scratch_shapes=[
            pltpu.VMEM(s_qkv.shape[::-1], BF16),
            pltpu.VMEM(s_out.shape, BF16),
            pltpu.VMEM(t_qkv.shape[::-1], BF16),
            pltpu.VMEM(t_out.shape, BF16),
            pltpu.VMEM((2 * width, LANES), BF16),
            pltpu.VMEM((LANES, 2 * width), BF16),
            *[pltpu.VMEM((slots, padded), BF16)] * 3,
            *[pltpu.VMEM((span, padded), BF16)] * 3,
            pltpu.VMEM((slots, model), BF16),
            pltpu.VMEM((slots, model), BF16),
            pltpu.VMEM((2, span, model), BF16),
            pltpu.VMEM((2, span, width), BF16),
            pltpu.VMEM((slots, width), BF16),
            pltpu.VMEM((8, LANES), I32),
            pltpu.VMEM((n, 8, LANES), I32),
            pltpu.VMEM((NBLK, span), F32),
            dma((4,)),
            dma((2, third)),
            dma((n,)),
            dma((3, third)),
            dma((2, n)),
            dma((2, n)),
            dma((3 * third,)),
        ],
        compiler_params=pltpu.CompilerParams(
            collective_id=0, has_side_effects=True, vmem_limit_bytes=58 * 1024 * 1024
        ),
        cost_estimate=pl.CostEstimate(
            flops=6_000_000_000, bytes_accessed=13_000_000, transcendentals=2_400_000
        ),
    )(
        cam_len,
        view_mask,
        time_mask,
        video,
        s_gain,
        t_gain,
        qk_gain,
        s_qkv.T,
        s_out,
        t_qkv.T,
        t_out,
    )


def solution(mesh):
    placed = (P(("groups", "tm"), None, None), P(("groups", "tm"), None)) + (P(),) * 9
    return jax.shard_map(
        functools.partial(body, mesh.shape["tm"]),
        mesh=mesh,
        in_specs=placed,
        out_specs=P(("groups", "tm"), None, None),
        check_vma=False,
    )
```

```python
import functools

import jax
import jax.numpy as jnp
from jax import lax
from jax.experimental import pallas as pl
from jax.experimental.pallas import tpu as pltpu
from jax.sharding import PartitionSpec as P

HEADS = 8
HD = 72
CAMS = 6
NBLK = 8
UNIT = 16
ROWS = 128
LANES = 128
EPS = 1e-06
SCALE = HD ** (-0.5)
NEG = -1e30
F32, BF16, I32 = jnp.float32, jnp.bfloat16, jnp.int32


def normalize(values, gain):
    average = jnp.mean(values, -1, keepdims=True)
    centred = values - average
    spread = jnp.mean(centred * centred, -1, keepdims=True)
    return (centred * lax.rsqrt(spread + EPS) * gain).astype(BF16)


def project(rows, weight, gain, sums, spreads, q_ref, k_ref, v_ref, at):
    width = HEADS * HD
    packed = lax.dot_general(
        rows, weight[...], (((1,), (1,)), ((), ())), preferred_element_type=F32
    )
    qk = packed[:, : 2 * width]
    total = jnp.dot((qk * qk).astype(BF16), sums[...], preferred_element_type=F32)
    inverse = lax.rsqrt(total * (1.0 / HD) + EPS)
    high = inverse.astype(BF16).astype(F32)
    lane = lax.broadcasted_iota(I32, inverse.shape, 1)
    both = jnp.where(lane < 2 * HEADS, high, inverse - high).astype(BF16)
    spread = jnp.dot(both, spreads[...], preferred_element_type=F32)
    normed = (qk * spread * gain).astype(BF16)
    q_ref[at, :width] = normed[:, :width]
    k_ref[at, :width] = normed[:, width:]
    v_ref[at, :width] = packed[:, 2 * width :].astype(BF16)


def attend(q_ref, k_ref, v_ref, q_at, k_at, bias):
    tiles = [None] * (-(-HEADS * HD // LANES))
    group = HEADS if bias.shape[1] <= 512 else 2
    for begin in range(0, HEADS, group):
        views = []
        for head in range(begin, begin + group):
            first, last = head * HD // LANES, ((head + 1) * HD - 1) // LANES
            lane = lax.broadcasted_iota(I32, (1, (last + 1 - first) * LANES), 1) + first * LANES
            inside = (lane >= head * HD) & (lane < (head + 1) * HD)
            views.append((first, last, slice(first * LANES, (last + 1) * LANES), inside))
        scores = []
        for _, _, window, inside in views:
            queries = q_ref[q_at, window] * jnp.where(inside, 1.0, 0.0).astype(BF16)
            scores.append(
                lax.dot_general(
                    queries,
                    k_ref[k_at, window],
                    (((1,), (1,)), ((), ())),
                    preferred_element_type=F32,
                )
            )
        weights = []
        for score in scores:
            score = score * SCALE + bias
            exponent = jnp.exp(score - jnp.max(score, -1, keepdims=True))
            weights.append(
                (exponent * (1.0 / jnp.sum(exponent, -1, keepdims=True))).astype(BF16)
            )
        for weight, (first, last, window, inside) in zip(weights, views):
            part = jnp.dot(weight, v_ref[k_at, window], preferred_element_type=F32)
            part = jnp.where(inside, part, 0.0)
            for tile in range(first, last + 1):
                piece = part[:, (tile - first) * LANES : (tile - first + 1) * LANES]
                tiles[tile] = piece if tiles[tile] is None else tiles[tile] + piece
    return jnp.concatenate(tiles, 1).astype(BF16)


def kernel(
    n,
    cam_len,
    view_mask,
    time_mask,
    video,
    s_gain,
    t_gain,
    qk_gain,
    s_qkv_hbm,
    s_out_hbm,
    t_qkv_hbm,
    t_out_hbm,
    out,
    s_qkv,
    s_out,
    t_qkv,
    t_out,
    sums,
    spreads,
    sq,
    sk,
    sv,
    tq,
    tk,
    tv,
    after,
    sending,
    received,
    attended,
    returned,
    cam_row,
    cams_all,
    links,
    weight_sem,
    cam_send,
    cam_recv,
    go_send,
    go_recv,
    back_send,
    back_recv,
):
    slots, model = after.shape
    width = HEADS * HD
    third = slots // (3 * UNIT)
    stride = (n // 2) // third
    me = lax.axis_index("tm")
    my_chip, my_core = me // 2, me % 2
    my_item = my_chip // stride
    working = (my_chip % stride) == 0
    my_units = jnp.where(working, 2 - my_core, 0)
    other = lax.rem(me + 1, n)

    loads = [
        pltpu.make_async_copy(src, dst, weight_sem.at[i])
        for i, (src, dst) in enumerate(
            ((s_qkv_hbm, s_qkv), (s_out_hbm, s_out), (t_qkv_hbm, t_qkv), (t_out_hbm, t_out))
        )
    ]
    loads[0].start()

    barrier = pltpu.get_barrier_semaphore()

    def greet(step, carry):
        peer = lax.rem(me + step, n)
        pl.semaphore_signal(
            barrier, inc=1, device_id={"tm": peer}, device_id_type=pl.DeviceIdType.MESH
        )
        return carry

    lax.fori_loop(1, n, greet, 0)

    entry = lax.broadcasted_iota(I32, sums.shape, 0)
    head = lax.broadcasted_iota(I32, sums.shape, 1)
    head = jnp.where(head < 2 * HEADS, head, head - 2 * HEADS) * HD
    sums[...] = jnp.where((entry >= head) & (entry < head + HD), 1.0, 0.0).astype(BF16)
    entry = lax.broadcasted_iota(I32, spreads.shape, 1)
    head = lax.broadcasted_iota(I32, spreads.shape, 0)
    head = jnp.where(head < 2 * HEADS, head, head - 2 * HEADS) * HD
    spreads[...] = jnp.where((entry >= head) & (entry < head + HD), 1.0, 0.0).astype(BF16)
    lane = lax.broadcasted_iota(I32, cam_row.shape, 1)
    lengths = jnp.zeros(cam_row.shape, I32)
    for cam in range(CAMS):
        lengths = jnp.where(lane == cam, cam_len[0, cam], lengths)
    cam_row[...] = lengths
    for ref in (sq, sk, sv, tq, tk, tv):
        ref[:, width:] = jnp.zeros((ref.shape[0], ref.shape[1] - width), BF16)

    def qk_row(first):
        pair = [qk_gain[first + i : first + i + 1, :] for i in range(2)]
        return jnp.concatenate([pair[0]] * HEADS + [pair[1]] * HEADS, 1)

    def to_normed(step, carry):
        at = pl.ds(pl.multiple_of(step * 64, 64), 64)
        sending[at, :] = normalize(video[0, at, :].astype(F32), s_gain[...][None, :])
        return carry

    lax.fori_loop(0, slots // 64, to_normed, 0, unroll=True)
    loads[0].wait()
    for load in loads[1:]:
        load.start()

    project(sending[...], s_qkv, qk_row(0), sums, spreads, sq, sk, sv, slice(None))

    pl.semaphore_wait(barrier, n - 1)

    def device_of(item, core):
        return item * (2 * stride) + core

    def cam_copy(item, core, frame):
        return pltpu.make_async_remote_copy(
            src_ref=cam_row,
            dst_ref=cams_all.at[frame],
            send_sem=cam_send.at[core, item],
            recv_sem=cam_recv.at[frame],
            device_id={"tm": device_of(item, core)},
            device_id_type=pl.DeviceIdType.MESH,
        )

    for core in range(2):

        def send_cams(item, carry):
            @pl.when(device_of(item, core) != me)
            def _():
                cam_copy(item, core, me).start()

            return carry

        lax.fori_loop(0, third, send_cams, 0)

    def go_copy(part, item, frame):
        core, slot = (1, 0) if part == 1 else (0, part // 2)
        at = pl.ds(pl.multiple_of((part * third + item) * UNIT, UNIT), UNIT)
        return pltpu.make_async_remote_copy(
            src_ref=sending.at[at],
            dst_ref=received.at[slot, pl.ds(pl.multiple_of(frame * UNIT, UNIT), UNIT)],
            send_sem=go_send.at[part, item],
            recv_sem=go_recv.at[slot, frame],
            device_id={"tm": device_of(item, core)},
            device_id_type=pl.DeviceIdType.MESH,
        )

    camera = lax.broadcasted_iota(I32, (1, slots), 1)
    tile = slots // CAMS
    length = jnp.zeros((1, slots), I32)
    for cam in range(CAMS):
        length = jnp.where(
            (camera >= cam * tile) & (camera < (cam + 1) * tile), cam_len[0, cam] + cam * tile, length
        )
    live = camera < length

    def camera_bias(query):
        seen = jnp.zeros((1, slots), I32)
        for cam in range(CAMS):
            mark = jnp.int32(1) if cam == query else view_mask[query, cam]
            seen = jnp.where((camera >= cam * tile) & (camera < (cam + 1) * tile), mark, seen)
        row = jnp.where((seen > 0) & live, 0.0, NEG)
        return jnp.broadcast_to(row, (tile, slots))

    loads[1].wait()
    per = ROWS // tile
    for part in range(3):
        at = pl.ds(part * ROWS, ROWS)
        bias = jnp.concatenate([camera_bias(part * per + i) for i in range(per)], 0)
        heads = attend(sq, sk, sv, at, slice(None), bias)[:, :width]
        mixed = jnp.dot(heads, s_out[...], preferred_element_type=F32)
        after_space = (video[0, at, :].astype(F32) + mixed).astype(BF16)
        after[at, :] = after_space
        sending[at, :] = normalize(after_space.astype(F32), t_gain[...][None, :])
        core, slot = (1, 0) if part == 1 else (0, part // 2)

        def send_part(step, carry):
            near = third // 2
            half = my_item // near
            half = jnp.where(step < near, 1 - half, half)
            item = half * near + lax.rem(my_item + step, near)

            @pl.when(device_of(item, core) != me)
            def _():
                go_copy(part, item, me).start()

            return carry

        lax.fori_loop(0, third, send_part, 0)

        @pl.when(working & (my_core == core))
        def _():
            own = pl.ds(pl.multiple_of((part * third + my_item) * UNIT, UNIT), UNIT)
            received[slot, pl.ds(pl.multiple_of(me * UNIT, UNIT), UNIT), :] = sending[own, :]

    loads[2].wait()

    @pl.when(working)
    def _():
        cams_all[me] = cam_row[...]

        def cam_arrived(step, carry):
            cam_copy(0, 0, lax.rem(me + step, n)).wait_recv()
            return carry

        lax.fori_loop(1, n, cam_arrived, 0)

    span = n * UNIT
    block = span // NBLK

    def unit_of(slot):
        part = jnp.where(my_core == 1, 1, 2 * slot)
        return part * third + my_item

    def back_copy(slot, frame, unit):
        return pltpu.make_async_remote_copy(
            src_ref=attended.at[slot, pl.ds(pl.multiple_of(frame * UNIT, UNIT), UNIT)],
            dst_ref=returned.at[pl.ds(pl.multiple_of(unit * UNIT, UNIT), UNIT)],
            send_sem=back_send.at[slot, frame],
            recv_sem=back_recv.at[unit],
            device_id={"tm": frame},
            device_id_type=pl.DeviceIdType.MESH,
        )

    def work(slot, carry):
        unit = unit_of(slot)

        def arrived(step, inner):
            frame = lax.rem(me + step, n)
            pltpu.make_async_remote_copy(
                src_ref=sending.at[pl.ds(0, UNIT)],
                dst_ref=received.at[slot, pl.ds(pl.multiple_of(frame * UNIT, UNIT), UNIT)],
                send_sem=go_send.at[0, 0],
                recv_sem=go_recv.at[slot, frame],
                device_id={"tm": other},
                device_id_type=pl.DeviceIdType.MESH,
            ).wait_recv()
            return inner

        lax.fori_loop(1, n, arrived, 0)

        def heads_of(step, inner):
            at = pl.ds(pl.multiple_of(step * 2 * ROWS, ROWS), 2 * ROWS)
            project(received[slot, at, :], t_qkv, qk_row(2), sums, spreads, tq, tk, tv, at)
            return inner

        lax.fori_loop(0, span // (2 * ROWS), heads_of, 0)

        per_camera = tile // UNIT
        cam_lane = lax.broadcasted_iota(I32, (n, LANES), 1)
        cam_col = jnp.sum(
            jnp.where(cam_lane == unit // per_camera, cams_all[:, 0, :], 0), 1, keepdims=True
        )
        key = lax.broadcasted_iota(I32, (n, span), 1)
        begin = lax.broadcasted_iota(I32, (n, span), 0) * UNIT
        mine = (key >= begin) & (key < begin + UNIT)
        spot = key - begin + lax.rem(unit, per_camera) * UNIT
        usable = jnp.sum(jnp.where(mine & (spot < cam_col), 1.0, 0.0), 0, keepdims=True)
        column = lax.broadcasted_iota(I32, (1, span), 1)
        for query in range(NBLK):
            marks = jnp.zeros((1, span), I32)
            for other_block in range(NBLK):
                inside = (column >= other_block * block) & (column < (other_block + 1) * block)
                marks = jnp.where(inside, time_mask[query, other_block], marks)
            links[query : query + 1, :] = jnp.where(marks > 0, usable, 0.0)

        pieces = span // ROWS
        far = jnp.where(me < n // 2, pieces // 2, 0)

        def mix(step, inner):
            piece = lax.rem(step + far, pieces)
            at = pl.ds(pl.multiple_of(piece * ROWS, ROWS), ROWS)
            row = lax.broadcasted_iota(I32, (ROWS, 1), 0) + piece * ROWS
            mark = jnp.zeros((ROWS, span), F32)
            for query in range(NBLK):
                inside = (row >= query * block) & (row < (query + 1) * block)
                mark = jnp.where(inside, links[query : query + 1, :], mark)
            row_frame, column_frame = row // UNIT, column // UNIT
            same_slot = (row - row_frame * UNIT) == (column - column_frame * UNIT)
            earlier = (row_frame > column_frame) & (mark > 0.5)
            bias = jnp.where(same_slot & ((row_frame == column_frame) | earlier), 0.0, NEG)
            attended[slot, at, :] = attend(tq, tk, tv, at, slice(None), bias)[:, :width]
            frames = ROWS // UNIT

            def send_back(turn, deeper):
                frame = piece * frames + lax.rem(me + turn, frames)

                @pl.when(frame != me)
                def _():
                    back_copy(slot, frame, unit).start()

                return deeper

            return lax.fori_loop(0, frames, send_back, inner)

        lax.fori_loop(0, pieces, mix, 0)
        own = pl.ds(pl.multiple_of(me * UNIT, UNIT), UNIT)
        returned[pl.ds(pl.multiple_of(unit * UNIT, UNIT), UNIT), :] = attended[slot, own, :]
        return carry

    lax.fori_loop(0, my_units, work, 0)

    loads[3].wait()
    for part in range(3):
        core = 1 if part == 1 else 0

        def came_back(item, carry):
            @pl.when(device_of(item, core) != me)
            def _():
                unit = part * third + item
                pltpu.make_async_remote_copy(
                    src_ref=attended.at[0, pl.ds(0, UNIT)],
                    dst_ref=returned.at[pl.ds(pl.multiple_of(unit * UNIT, UNIT), UNIT)],
                    send_sem=back_send.at[0, 0],
                    recv_sem=back_recv.at[unit],
                    device_id={"tm": other},
                    device_id_type=pl.DeviceIdType.MESH,
                ).wait_recv()

            return carry

        lax.fori_loop(0, third, came_back, 0)
        at = pl.ds(part * ROWS, ROWS)
        mixed = jnp.dot(returned[at, :], t_out[...], preferred_element_type=F32).astype(BF16)
        out[0, at, :] = (after[at, :].astype(F32) + mixed.astype(F32)).astype(BF16)

    for core in range(2):

        def cams_sent(item, carry):
            @pl.when(device_of(item, core) != me)
            def _():
                cam_copy(item, core, me).wait_send()

            return carry

        lax.fori_loop(0, third, cams_sent, 0)
    for part in range(3):
        core = 1 if part == 1 else 0

        def part_sent(item, carry):
            @pl.when(device_of(item, core) != me)
            def _():
                go_copy(part, item, me).wait_send()

            return carry

        lax.fori_loop(0, third, part_sent, 0)

    def unit_sent(slot, carry):
        def frame_sent(step, inner):
            back_copy(slot, lax.rem(me + step, n), unit_of(slot)).wait_send()
            return inner

        return lax.fori_loop(1, n, frame_sent, carry)

    lax.fori_loop(0, my_units, unit_sent, 0)


def body(
    n, video, cam_len, view_mask, time_mask, s_gain, t_gain, s_qkv, s_out, t_qkv, t_out, qk_gain
):
    _, slots, model = video.shape
    width = HEADS * HD
    padded = -(-width // LANES) * LANES
    span = n * UNIT
    third = slots // (3 * UNIT)
    smem = pl.BlockSpec(memory_space=pltpu.SMEM)
    vmem = pl.BlockSpec(memory_space=pltpu.VMEM)
    hbm = pl.BlockSpec(memory_space=pl.ANY)
    dma = pltpu.SemaphoreType.DMA
    return pl.pallas_call(
        functools.partial(kernel, n),
        out_shape=jax.ShapeDtypeStruct(video.shape, BF16),
        in_specs=[smem] * 3 + [vmem] * 4 + [hbm] * 4,
        out_specs=vmem,
        scratch_shapes=[
            pltpu.VMEM(s_qkv.shape[::-1], BF16),
            pltpu.VMEM(s_out.shape, BF16),
            pltpu.VMEM(t_qkv.shape[::-1], BF16),
            pltpu.VMEM(t_out.shape, BF16),
            pltpu.VMEM((2 * width, LANES), BF16),
            pltpu.VMEM((LANES, 2 * width), BF16),
            *[pltpu.VMEM((slots, padded), BF16)] * 3,
            *[pltpu.VMEM((span, padded), BF16)] * 3,
            pltpu.VMEM((slots, model), BF16),
            pltpu.VMEM((slots, model), BF16),
            pltpu.VMEM((2, span, model), BF16),
            pltpu.VMEM((2, span, width), BF16),
            pltpu.VMEM((slots, width), BF16),
            pltpu.VMEM((8, LANES), I32),
            pltpu.VMEM((n, 8, LANES), I32),
            pltpu.VMEM((NBLK, span), F32),
            dma((4,)),
            dma((2, third)),
            dma((n,)),
            dma((3, third)),
            dma((2, n)),
            dma((2, n)),
            dma((3 * third,)),
        ],
        compiler_params=pltpu.CompilerParams(
            collective_id=0, has_side_effects=True, vmem_limit_bytes=58 * 1024 * 1024
        ),
        cost_estimate=pl.CostEstimate(
            flops=6_000_000_000, bytes_accessed=13_000_000, transcendentals=2_400_000
        ),
    )(
        cam_len,
        view_mask,
        time_mask,
        video,
        s_gain,
        t_gain,
        qk_gain,
        s_qkv.T,
        s_out,
        t_qkv.T,
        t_out,
    )


def solution(mesh):
    placed = (P(("groups", "tm"), None, None), P(("groups", "tm"), None)) + (P(),) * 9
    return jax.shard_map(
        functools.partial(body, mesh.shape["tm"]),
        mesh=mesh,
        in_specs=placed,
        out_specs=P(("groups", "tm"), None, None),
        check_vma=False,
    )
```
